32 devices in a mesh: groups: 2 (over y), area: 4 (over z), neuron: 4 (over x, core).
Axes of the slice: x: 2, y: 2, z: 4, core: 2. Of those that a mesh axis runs over, the one named last changes fastest.
Arguments:
- window: bfloat16 [32, 16, 32768], P(None, 'groups', ('area', 'neuron')), parts along dimension 1, may hold values from -6 to 6
- err_grad: float32 [16, 16, 32768], P(None, 'groups', ('area', 'neuron')), parts along dimension 1, may hold values from -6 to 6
- surrogate: float32 [16, 16, 32768], P(None, 'groups', ('area', 'neuron')), parts along dimension 1, may hold values from 0 to 0.5
- lv_end: float32 [16, 32768], P('groups', ('area', 'neuron')), parts along dimension 0, may hold values from -6 to 6
- la_end: float32 [16, 32768], P('groups', ('area', 'neuron')), parts along dimension 0, may hold values from -6 to 6
- alpha: float32 [32768], P(('area', 'neuron')), may hold values from 0.8 to 0.99
- rho: float32 [32768], P(('area', 'neuron')), may hold values from 0.9 to 0.999
- beta: float32 [32768], P(('area', 'neuron')), may hold values from 0.3 to 2
- weights: bfloat16 [4, 4, 64, 4, 128, 128], P(None, 'area', 'neuron'), may hold values from -0.25 to 0.25
- block_index: int32 [4, 4, 64, 4], P(None, 'area', 'neuron'), may hold values from 0 to 63, as said below
- delays: int32 [4, 4], replicated, may hold values from 16 to 31, as said below
Outputs:
- cur_adjoint: bfloat16 [16, 16, 32768], P(None, 'groups', ('area', 'neuron')), parts along dimension 1
- lv_start: float32 [16, 32768], P('groups', ('area', 'neuron')), parts along dimension 0
- la_start: float32 [16, 32768], P('groups', ('area', 'neuron')), parts along dimension 0
The draws below stay inside these ranges and needn't reach their ends.
There are 2 independent parts, one for each index of `groups`. The reference program is written for one: setup_inputs(seed, part) draws one part's arguments, and reference() takes and returns one part's arrays. A program takes and returns all parts, laid end to end along the dimension named above; an argument that names none is the same for every part. Nothing has to cross between parts.
Inputs may be any that keep to these rules, and one draw needn't show every extreme that they name: `delays`: every entry lies in 16 to 31 and both ends occur. `block_index`: both ends occur.
All inputs are finite; a program needn't handle non-finite values.
Results may differ from the reference program's by a relative error of at most 0.001.
Values may be sent and summed in bfloat16 or wider, within the bound.
A program may use at most 64 MiB of HBM per device.

```python
import math
import jax
import jax.numpy as jnp
from jax import lax

K = 16
B = 8
BLK = 128
NNZ = 4
ROUNDS = 4
AREAS = 4
NA = 8192
NBA = 64
NEUR = 32768
N_AREA = 4


def draw_block_index(key, part):
    values = jax.random.randint(jax.random.fold_in(key, 11), (ROUNDS, AREAS, NBA, NNZ), 0, NBA)
    values = values.at[0, 0, 0, 0].set(NBA - 1)
    values = values.at[0, 0, 0, 1].set(0)
    return values.astype(jnp.int32)


def draw_delays(key, part):
    values = jax.random.randint(jax.random.fold_in(key, 23), (ROUNDS, AREAS), K, 2 * K)
    values = values.at[0, 0].set(2 * K - 1)
    values = values.at[0, 1].set(K)
    return values.astype(jnp.int32)


def level_of(own_key, dims, pieces, least, largest):
    def one(dim, parts):
        draws = jax.random.uniform(jax.random.fold_in(jax.random.fold_in(own_key, 6), dim), (parts,), jnp.float32, least / len(pieces), largest / len(pieces))
        return jnp.repeat(jnp.exp(draws), dims[dim] // parts).reshape((-1,) + (1,) * (len(dims) - dim - 1))

    gain = one(*pieces[0])
    for cut in pieces[1:]:
        gain = gain * one(*cut)
    return gain


def scatter_about(own_key, extent, scale, most, pieces=(), held_as=jnp.bfloat16):
    values = jax.random.normal(own_key, extent, jnp.float32) * scale
    if len(pieces) > 0:
        values = level_of(own_key, extent, pieces, -0.22, 0.18) * values
    return jnp.clip(values, min=-most, max=most).astype(held_as)


def setup_inputs(seed: int = 0, part: int = 0) -> dict:
    key_list = jax.random.split(jax.random.key(seed), 12)
    part_splits = jax.random.split(jax.random.fold_in(key_list[11], part), 12)
    return {
        "window": scatter_about(part_splits[0], (2 * K, B, NEUR), 1.0, 6.0, ((2, 16),)),
        "err_grad": scatter_about(part_splits[1], (K, B, NEUR), 1.0, 6.0, ((2, 16),), jnp.float32),
        "surrogate": jnp.clip(0.5 * jax.random.uniform(part_splits[2], (K, B, NEUR), jnp.float32) ** level_of(part_splits[2], (K, B, NEUR), ((2, 16),), -0.2, 0.2), 0.0, 0.5),
        "lv_end": scatter_about(part_splits[3], (B, NEUR), 1.0, 6.0, ((1, 16),), jnp.float32),
        "la_end": scatter_about(part_splits[4], (B, NEUR), 1.0, 6.0, ((1, 16),), jnp.float32),
        "alpha": jnp.clip(jnp.exp(math.log(0.99) - 0.2130932 * jax.random.uniform(key_list[5], (NEUR,), jnp.float32) ** level_of(key_list[5], (NEUR,), ((0, 16),), -0.2, 0.2)), 0.8, 0.99),
        "rho": jnp.clip(jnp.exp(math.log(0.999) - 0.10436005 * jax.random.uniform(key_list[6], (NEUR,), jnp.float32) ** level_of(key_list[6], (NEUR,), ((0, 16),), -0.2, 0.2)), 0.9, 0.999),
        "beta": jnp.clip(jnp.exp(math.log(2.0) - 1.89712 * jax.random.uniform(key_list[7], (NEUR,), jnp.float32) ** level_of(key_list[7], (NEUR,), ((0, 16),), -0.2, 0.2)), 0.3, 2.0),
        "weights": scatter_about(key_list[8], (ROUNDS, AREAS, NBA, NNZ, BLK, BLK), (NNZ * BLK) ** -0.5, 0.25, ((1, 4), (2, 4))),
        "block_index": draw_block_index(jax.random.fold_in(key_list[11], 71), part),
        "delays": draw_delays(jax.random.fold_in(key_list[11], 71), part),
    }


def adjoint_scan(err_grad, surrogate, rec, lv_end, la_end, alpha, rho, beta):
    def step(carry, inputs):
        lv_now, la_now = carry
        error_t, surr_t, rec_t = inputs
        total = error_t + rec_t - lv_now + la_now
        lv_next = alpha * lv_now + surr_t * total
        la_next = rho * la_now - beta * surr_t * total
        return (lv_next, la_next), lv_now.astype(jnp.bfloat16)

    (lv_start, la_start), currents = lax.scan(step, (lv_end, la_end), (err_grad, surrogate, rec), reverse=True)
    return currents, lv_start, la_start


def reference(window, err_grad, surrogate, lv_end, la_end, alpha, rho, beta, weights, block_index, delays):
    levels = N_AREA.bit_length() - 1
    area_ids = jnp.arange(N_AREA, dtype=jnp.int32)
    split = window.reshape(2 * K, B, N_AREA, NA)
    rec = jnp.zeros((N_AREA, K * B, NA), jnp.float32)
    for rnd in range(ROUNDS):
        partners = jnp.bitwise_xor(area_ids, 1 << (rnd % levels))

        def one_area(area):
            partner = partners[area]
            start = (delays[rnd, area] - K).astype(jnp.int32)
            zero = jnp.zeros((), jnp.int32)
            slab = lax.dynamic_slice(split, (start, zero, partner.astype(jnp.int32), zero), (K, B, 1, NA))
            slab = slab.reshape(K * B, NBA, BLK)
            picked = jnp.take(slab, block_index[rnd, area], axis=1)
            blocks = weights[rnd, area]
            out = jnp.einsum("rjkc,jkcd->rjd", picked.astype(jnp.float32), blocks.astype(jnp.float32))
            return out.reshape(K * B, NA)

        rec = rec + lax.map(one_area, area_ids)
    rec = jnp.transpose(rec, (1, 0, 2)).reshape(K, B, N_AREA * NA)
    return adjoint_scan(err_grad, surrogate, rec, lv_end, la_end, alpha, rho, beta)
```

```python
import functools

import jax
import jax.numpy as jnp
from jax import lax
from jax.experimental import pallas as pl
from jax.experimental.pallas import tpu as pltpu
from jax.sharding import PartitionSpec as P

MESH = pl.DeviceIdType.MESH
CHUNK = 2


def kernel(
    rounds_of,
    spans,
    delays_ref,
    index_ref,
    window,
    err_hbm,
    surr_hbm,
    lv_hbm,
    la_hbm,
    alpha_ref,
    rho_ref,
    beta_ref,
    weights_hbm,
    cur_ref,
    lv_ref,
    la_ref,
    *scratch,
):
    partners = len(rounds_of)
    held = scratch[:partners]
    own, weights, err, surr, lv_in, la_in, rec, send, recv, local, staged = scratch[partners:]
    me = lax.axis_index("neuron")
    area = lax.axis_index("area")
    n = lax.axis_size("neuron")
    levels = n.bit_length() - 1
    steps, batch, neurons = err.shape
    blocks, nnz, side = weights.shape[1:4]
    used = 2 * steps - 1

    loads = [
        pltpu.make_async_copy(src, dst, local.at[i])
        for i, (src, dst) in enumerate(
            (
                (weights_hbm.at[:, 0], weights),
                (err_hbm, err),
                (surr_hbm, surr),
                (lv_hbm, lv_in),
                (la_hbm, la_in),
            )
        )
    ]

    stage = [
        pltpu.make_async_copy(
            window.at[pl.ds(0, used), :, pl.ds(b * side, side)],
            own.at[b, pl.ds(0, used)],
            staged.at[b],
        )
        for b in range(blocks)
    ]
    for copy in stage:
        copy.start()

    barrier = pltpu.get_barrier_semaphore()
    for bit, _ in rounds_of:
        pl.semaphore_signal(
            barrier, inc=1, device_id={"area": area ^ (1 << bit)}, device_id_type=MESH
        )
    for bit in range(levels):
        pl.semaphore_signal(
            barrier, inc=1, device_id={"neuron": me ^ (1 << bit)}, device_id_type=MESH
        )
    pl.semaphore_wait(barrier, partners + levels)

    def entry(p, q):
        first, size = spans[q]
        where = held[p].at[pl.ds(me * blocks + first, size), pl.ds(0, used)]
        return pltpu.make_async_remote_copy(
            src_ref=own.at[pl.ds(first, size), pl.ds(0, used)],
            dst_ref=where,
            send_sem=send.at[p, q, 0],
            recv_sem=recv.at[p, q, 0],
            device_id={"area": area ^ (1 << rounds_of[p][0])},
            device_id_type=MESH,
        )

    def forward(p, q, origin, bit):
        first, size = spans[q]
        where = held[p].at[pl.ds((me ^ origin) * blocks + first, size), pl.ds(0, used)]
        there = origin ^ (1 << bit)
        return pltpu.make_async_remote_copy(
            src_ref=where,
            dst_ref=where,
            send_sem=send.at[p, q, there],
            recv_sem=recv.at[p, q, there],
            device_id={"neuron": me ^ (1 << bit)},
            device_id_type=MESH,
        )

    def arrival(p, q, origin):
        first, size = spans[q]
        where = held[p].at[pl.ds((me ^ origin) * blocks + first, size), pl.ds(0, used)]
        return pltpu.make_async_remote_copy(
            src_ref=where,
            dst_ref=where,
            send_sem=send.at[p, q, origin],
            recv_sem=recv.at[p, q, origin],
            device_id={"neuron": me ^ 1},
            device_id_type=MESH,
        )

    started = []
    order = [(p, q) for q in range(len(spans)) for p in reversed(range(partners))]
    ready = 0
    for p, q in order:
        first, size = spans[q]
        while ready < first + size:
            stage[ready].wait()
            ready += 1
        copy = entry(p, q)
        copy.start()
        started.append(copy)
    for copy in loads:
        copy.start()

    def pass_on(p, q, origin, below):
        for bit in reversed(range(below)):
            copy = forward(p, q, origin, bit)
            copy.start()
            started.append(copy)

    relays = [d for d in range(2, n, 2)]
    for i in range(len(order) + 1):
        if i < len(order):
            p, q = order[i]
            entry(p, q).wait_recv()
            pass_on(p, q, 0, levels)
        if i >= 1:
            p, q = order[i - 1]
            for d in relays:
                arrival(p, q, d).wait_recv()
                pass_on(p, q, d, (d & -d).bit_length() - 1)
    for p, q in order:
        for d in range(1, n, 2):
            arrival(p, q, d).wait_recv()
    for copy in loads:
        copy.wait()

    def column(j, carry):
        total = jnp.zeros((steps * batch, side), jnp.float32)
        for p, (_, rounds) in enumerate(rounds_of):
            for r in rounds:
                start = jnp.maximum(delays_ref[r, area] - steps, 0)
                parts = []
                for k in range(nnz):
                    idx = index_ref[r, 0, j, k]
                    got = held[p][idx, pl.ds(start, steps)]
                    parts.append(got.reshape(steps * batch, side))
                left = jnp.concatenate(parts, axis=1)
                right = weights[r, j].reshape(nnz * side, side)
                total += jnp.dot(left, right, preferred_element_type=jnp.float32)
        at = pl.ds(pl.multiple_of(j * side, side), side)
        rec[:, :, at] = total.reshape(steps, batch, side)
        return carry

    lax.fori_loop(0, blocks, column, 0)

    width = 4 * side

    def scan(c, carry):
        at = pl.ds(pl.multiple_of(c * width, width), width)
        alpha = jnp.broadcast_to(alpha_ref[:, at], (batch, width))
        rho = jnp.broadcast_to(rho_ref[:, at], (batch, width))
        beta = jnp.broadcast_to(beta_ref[:, at], (batch, width))
        lv = lv_in[:, at]
        la = la_in[:, at]
        for t in reversed(range(steps)):
            total = err[t, :, at] + rec[t, :, at] - lv + la
            cur_ref[t, :, at] = lv.astype(cur_ref.dtype)
            push = surr[t, :, at] * total
            lv = alpha * lv + push
            la = rho * la - beta * push
        lv_ref[:, at] = lv
        la_ref[:, at] = la
        return carry

    lax.fori_loop(0, neurons // width, scan, 0)
    for copy in started:
        copy.wait_send()


def per_device(
    window, err_grad, surrogate, lv_end, la_end, alpha, rho, beta, weights, block_index, delays
):
    steps, batch, neurons = err_grad.shape
    rounds = weights.shape[0]
    levels = lax.axis_size("area").bit_length() - 1
    n = lax.axis_size("neuron")
    rounds_of = [
        (bit, tuple(r for r in range(rounds) if r % levels == bit))
        for bit in range(min(levels, rounds))
    ]
    blocks, side = weights.shape[2], weights.shape[-1]
    spans = [(s, min(CHUNK, blocks - s)) for s in range(0, blocks, CHUNK)]
    partners = len(rounds_of)
    sems = (partners, len(spans), n)
    hbm = pl.BlockSpec(memory_space=pl.ANY)
    vmem = pl.BlockSpec(memory_space=pltpu.VMEM)
    smem = pl.BlockSpec(memory_space=pltpu.SMEM)
    return pl.pallas_call(
        functools.partial(kernel, rounds_of, spans),
        out_shape=(
            jax.ShapeDtypeStruct(err_grad.shape, jnp.bfloat16),
            jax.ShapeDtypeStruct(lv_end.shape, jnp.float32),
            jax.ShapeDtypeStruct(la_end.shape, jnp.float32),
        ),
        in_specs=[smem, smem, hbm, hbm, hbm, hbm, hbm, vmem, vmem, vmem, hbm],
        out_specs=(vmem, vmem, vmem),
        scratch_shapes=[
            *[pltpu.VMEM((n * blocks, 2 * steps, batch, side), jnp.bfloat16)] * partners,
            pltpu.VMEM((blocks, 2 * steps, batch, side), jnp.bfloat16),
            pltpu.VMEM((rounds, *weights.shape[2:]), jnp.bfloat16),
            pltpu.VMEM(err_grad.shape, jnp.float32),
            pltpu.VMEM(err_grad.shape, jnp.float32),
            pltpu.VMEM(lv_end.shape, jnp.float32),
            pltpu.VMEM(lv_end.shape, jnp.float32),
            pltpu.VMEM(err_grad.shape, jnp.float32),
            pltpu.SemaphoreType.DMA(sems),
            pltpu.SemaphoreType.DMA(sems),
            pltpu.SemaphoreType.DMA((5,)),
            pltpu.SemaphoreType.DMA((blocks,)),
        ],
        compiler_params=pltpu.CompilerParams(
            collective_id=0, has_side_effects=True, vmem_limit_bytes=56 * 2**20
        ),
    )(
        delays,
        block_index,
        window,
        err_grad,
        surrogate,
        lv_end,
        la_end,
        alpha.reshape(1, -1),
        rho.reshape(1, -1),
        beta.reshape(1, -1),
        weights,
    )


def solution(mesh):
    neuron = P(("area", "neuron"))
    wide = P(None, "groups", ("area", "neuron"))
    row = P("groups", ("area", "neuron"))
    placed = (
        wide,
        wide,
        wide,
        row,
        row,
        neuron,
        neuron,
        neuron,
        P(None, "area", "neuron", None, None, None),
        P(None, "area", "neuron", None),
        P(),
    )
    return jax.shard_map(
        per_device,
        mesh=mesh,
        in_specs=placed,
        out_specs=(wide, row, row),
        check_vma=False,
    )
```

```python
import functools

import jax
import jax.numpy as jnp
from jax import lax
from jax.experimental import pallas as pl
from jax.experimental.pallas import tpu as pltpu
from jax.sharding import PartitionSpec as P

MESH = pl.DeviceIdType.MESH
CHUNK = 1
LAG = 4
GROUP = 4


def kernel(
    rounds_of,
    spans,
    delays_ref,
    index_ref,
    window,
    err_hbm,
    surr_hbm,
    lv_hbm,
    la_hbm,
    alpha_hbm,
    rho_hbm,
    beta_hbm,
    weights_hbm,
    cur_hbm,
    lv_hbm_out,
    la_hbm_out,
    *scratch,
):
    partners = len(rounds_of)
    held = scratch[:partners]
    (
        own, weights, err, surr, lv_in, la_in, alpha_ref, rho_ref, beta_ref,
        rec, cur_ref, lv_ref, la_ref, send, recv, local, staged, leave,
    ) = scratch[partners:]
    me = lax.axis_index("neuron")
    area = lax.axis_index("area")
    n = lax.axis_size("neuron")
    levels = n.bit_length() - 1
    steps, batch, neurons = err.shape
    blocks, nnz, side = weights.shape[1:4]
    used = 2 * steps - 1

    loads = [
        pltpu.make_async_copy(src, dst, local.at[i])
        for i, (src, dst) in enumerate(
            (
                (weights_hbm.at[:, 0], weights),
                (err_hbm, err),
                (surr_hbm, surr),
                (lv_hbm, lv_in),
                (la_hbm, la_in),
                (alpha_hbm, alpha_ref),
                (rho_hbm, rho_ref),
                (beta_hbm, beta_ref),
            )
        )
    ]

    stage = [
        pltpu.make_async_copy(
            window.at[pl.ds(0, used), :, pl.ds(b * side, side)],
            own.at[b, pl.ds(0, used)],
            staged.at[b],
        )
        for b in range(blocks)
    ]
    for copy in stage:
        copy.start()

    barrier = pltpu.get_barrier_semaphore()
    for bit, _ in rounds_of:
        pl.semaphore_signal(
            barrier, inc=1, device_id={"area": area ^ (1 << bit)}, device_id_type=MESH
        )
    for bit in range(levels):
        pl.semaphore_signal(
            barrier, inc=1, device_id={"neuron": me ^ (1 << bit)}, device_id_type=MESH
        )
    pl.semaphore_wait(barrier, partners + levels)

    def entry(p, q):
        first, size = spans[q]
        where = held[p].at[pl.ds(me * blocks + first, size), pl.ds(0, used)]
        return pltpu.make_async_remote_copy(
            src_ref=own.at[pl.ds(first, size), pl.ds(0, used)],
            dst_ref=where,
            send_sem=send.at[p, q, 0],
            recv_sem=recv.at[p, q, 0],
            device_id={"area": area ^ (1 << rounds_of[p][0])},
            device_id_type=MESH,
        )

    def forward(p, q, origin, bit):
        first, size = spans[q]
        where = held[p].at[pl.ds((me ^ origin) * blocks + first, size), pl.ds(0, used)]
        there = origin ^ (1 << bit)
        return pltpu.make_async_remote_copy(
            src_ref=where,
            dst_ref=where,
            send_sem=send.at[p, q, there],
            recv_sem=recv.at[p, q, there],
            device_id={"neuron": me ^ (1 << bit)},
            device_id_type=MESH,
        )

    def arrival(p, q, origin):
        first, size = spans[q]
        where = held[p].at[pl.ds((me ^ origin) * blocks + first, size), pl.ds(0, used)]
        return pltpu.make_async_remote_copy(
            src_ref=where,
            dst_ref=where,
            send_sem=send.at[p, q, origin],
            recv_sem=recv.at[p, q, origin],
            device_id={"neuron": me ^ 1},
            device_id_type=MESH,
        )

    started = []
    order = [(p, q) for q in range(len(spans)) for p in reversed(range(partners))]
    ready = 0
    for p, q in order:
        first, size = spans[q]
        while ready < first + size:
            stage[ready].wait()
            ready += 1
        copy = entry(p, q)
        copy.start()
        started.append(copy)
    for copy in loads:
        copy.start()

    def pass_on(p, q, origin, below):
        for bit in reversed(range(below)):
            copy = forward(p, q, origin, bit)
            copy.start()
            started.append(copy)

    relays = [d for d in range(2, n, 2)]
    for i in range(len(order) + LAG):
        if i < len(order):
            p, q = order[i]
            entry(p, q).wait_recv()
            pass_on(p, q, 0, levels)
        if i >= LAG:
            p, q = order[i - LAG]
            for d in relays:
                arrival(p, q, d).wait_recv()
                pass_on(p, q, d, (d & -d).bit_length() - 1)
    for p, q in order:
        for d in range(1, n, 2):
            arrival(p, q, d).wait_recv()
    for copy in loads:
        copy.wait()

    def column(j):
        total = jnp.zeros((steps * batch, side), jnp.float32)
        for p, (_, rounds) in enumerate(rounds_of):
            for r in rounds:
                start = jnp.maximum(delays_ref[r, area] - steps, 0)
                parts = []
                for k in range(nnz):
                    idx = index_ref[r, 0, k, j]
                    got = held[p][idx, pl.ds(start, steps)]
                    parts.append(got.reshape(steps * batch, side))
                left = jnp.concatenate(parts, axis=1)
                right = weights[r, j].reshape(nnz * side, side)
                total += jnp.dot(left, right, preferred_element_type=jnp.float32)
        at = pl.ds(pl.multiple_of(j * side, side), side)
        rec[:, :, at] = total.reshape(steps, batch, side)

    width = GROUP * side

    def leaving(c):
        at = pl.ds(pl.multiple_of(c * width, width), width)
        return [
            pltpu.make_async_copy(cur_ref.at[:, :, at], cur_hbm.at[:, :, at], leave.at[0, c]),
            pltpu.make_async_copy(lv_ref.at[:, at], lv_hbm_out.at[:, at], leave.at[1, c]),
            pltpu.make_async_copy(la_ref.at[:, at], la_hbm_out.at[:, at], leave.at[2, c]),
        ]

    def group(c, carry):
        for b in range(GROUP):
            column(c * GROUP + b)
        at = pl.ds(pl.multiple_of(c * width, width), width)
        alpha = jnp.broadcast_to(alpha_ref[:, at], (batch, width))
        rho = jnp.broadcast_to(rho_ref[:, at], (batch, width))
        beta = jnp.broadcast_to(beta_ref[:, at], (batch, width))
        lv = lv_in[:, at]
        la = la_in[:, at]
        for t in reversed(range(steps)):
            total = err[t, :, at] + rec[t, :, at] - lv + la
            cur_ref[t, :, at] = lv.astype(cur_ref.dtype)
            push = surr[t, :, at] * total
            lv = alpha * lv + push
            la = rho * la - beta * push
        lv_ref[:, at] = lv
        la_ref[:, at] = la
        for copy in leaving(c):
            copy.start()
        return carry

    lax.fori_loop(0, blocks // GROUP, group, 0)
    for c in range(blocks // GROUP):
        for copy in leaving(c):
            copy.wait()
    for copy in started:
        copy.wait_send()


def hand_on(*refs):
    *pairs, sem = refs
    half = len(pairs) // 2
    copies = [
        pltpu.make_async_copy(src, dst, sem.at[i])
        for i, (src, dst) in enumerate(zip(pairs[:half], pairs[half:]))
    ]
    for copy in copies:
        copy.start()
    for copy in copies:
        copy.wait()


def per_device(
    window, err_grad, surrogate, lv_end, la_end, alpha, rho, beta, weights, block_index, delays
):
    steps, batch, neurons = err_grad.shape
    rounds = weights.shape[0]
    levels = lax.axis_size("area").bit_length() - 1
    n = lax.axis_size("neuron")
    rounds_of = [
        (bit, tuple(r for r in range(rounds) if r % levels == bit))
        for bit in range(min(levels, rounds))
    ]
    blocks, side = weights.shape[2], weights.shape[-1]
    spans = [(s, min(CHUNK, blocks - s)) for s in range(0, blocks, CHUNK)]
    partners = len(rounds_of)
    sems = (partners, len(spans), n)
    hbm = pl.BlockSpec(memory_space=pl.ANY)
    smem = pl.BlockSpec(memory_space=pltpu.SMEM)
    outs = (
        jax.ShapeDtypeStruct(err_grad.shape, jnp.bfloat16),
        jax.ShapeDtypeStruct(lv_end.shape, jnp.float32),
        jax.ShapeDtypeStruct(la_end.shape, jnp.float32),
    )
    vector = pltpu.VMEM((1, neurons), jnp.float32)
    made = pl.pallas_call(
        functools.partial(kernel, rounds_of, spans),
        out_shape=outs,
        in_specs=[smem, smem, hbm, hbm, hbm, hbm, hbm, hbm, hbm, hbm, hbm],
        out_specs=(hbm, hbm, hbm),
        scratch_shapes=[
            *[pltpu.VMEM((n * blocks, 2 * steps, batch, side), jnp.bfloat16)] * partners,
            pltpu.VMEM((blocks, 2 * steps, batch, side), jnp.bfloat16),
            pltpu.VMEM((rounds, *weights.shape[2:]), jnp.bfloat16),
            pltpu.VMEM(err_grad.shape, jnp.float32),
            pltpu.VMEM(err_grad.shape, jnp.float32),
            pltpu.VMEM(lv_end.shape, jnp.float32),
            pltpu.VMEM(lv_end.shape, jnp.float32),
            vector,
            vector,
            vector,
            pltpu.VMEM(err_grad.shape, jnp.float32),
            pltpu.VMEM(err_grad.shape, jnp.bfloat16),
            pltpu.VMEM(lv_end.shape, jnp.float32),
            pltpu.VMEM(lv_end.shape, jnp.float32),
            pltpu.SemaphoreType.DMA(sems),
            pltpu.SemaphoreType.DMA(sems),
            pltpu.SemaphoreType.DMA((8,)),
            pltpu.SemaphoreType.DMA((blocks,)),
            pltpu.SemaphoreType.DMA((3, blocks // GROUP)),
        ],
        compiler_params=pltpu.CompilerParams(
            collective_id=0, has_side_effects=True, vmem_limit_bytes=56 * 2**20
        ),
    )(
        delays,
        jnp.transpose(block_index, (0, 1, 3, 2)),
        window,
        err_grad,
        surrogate,
        lv_end,
        la_end,
        alpha.reshape(1, -1),
        rho.reshape(1, -1),
        beta.reshape(1, -1),
        weights,
    )
    return pl.pallas_call(
        hand_on,
        out_shape=outs,
        in_specs=[pl.BlockSpec(memory_space=pltpu.VMEM)] * 3,
        out_specs=(hbm,) * 3,
        scratch_shapes=[pltpu.SemaphoreType.DMA((3,))],
    )(*made)


def solution(mesh):
    neuron = P(("area", "neuron"))
    wide = P(None, "groups", ("area", "neuron"))
    row = P("groups", ("area", "neuron"))
    placed = (
        wide,
        wide,
        wide,
        row,
        row,
        neuron,
        neuron,
        neuron,
        P(None, "area", "neuron", None, None, None),
        P(None, "area", "neuron", None),
        P(),
    )
    return jax.shard_map(
        per_device,
        mesh=mesh,
        in_specs=placed,
        out_specs=(wide, row, row),
        check_vma=False,
    )
```
